256 devices in a mesh: segment: 8 (over x, core), seq: 32 (over y, z).
Axes of the slice: x: 4, y: 4, z: 8, core: 2. Of those that a mesh axis runs over, the one named last changes fastest.
Arguments:
- hidden: bfloat16 [12288, 3072], P('seq'), may hold values from -6 to 6
- kv_cache: bfloat16 [8, 12288, 3072], P('segment', 'seq'), may hold values from -6 to 6
- q_weight: bfloat16 [8, 3072, 1536], P('segment', 'seq'), may hold values from -0.109375 to 0.109375
- o_weight: bfloat16 [8, 1536, 3072], P('segment', 'seq'), may hold values from -0.15625 to 0.15625
- mod_shift: float32 [8, 3072], P('segment'), may hold values from -3 to 3
- mod_scale: float32 [8, 3072], P('segment'), may hold values from -1.5 to 1.5
- mod_gate: float32 [8, 3072], P('segment'), may hold values from 0.5 to 2
- q_gain: float32 [8, 12], P('segment'), may hold values from 0.5 to 6
- tile_lists: int32 [32, 3], P('seq'), may hold values from 0 to 31, as said below
Outputs:
- layer_outputs: bfloat16 [8, 12288, 3072], P('segment', 'seq')
The draws below stay inside these ranges and needn't reach their ends.
Inputs may be any that keep to these rules, and one draw needn't show every extreme that they name: Row i of tile_lists begins with i; each of its other 2 entries is i - 1 or i + 1, a tile of the clip (entries may repeat).
All inputs are finite; a program needn't handle non-finite values.
Results may differ from the reference program's by a relative error of at most 0.034.
Values may be sent and summed in bfloat16 or wider, within the bound.
No kernel may reach another device: no remote copies, remote signals or barrier semaphores. Data moves between devices by JAX's collectives and lax.ppermute only.
A program may use at most 128 MiB of HBM per device.

```python
import math
import jax
import jax.numpy as jnp
from jax import lax

D = 3072
HDIM = 128
HEADS = 12
HD = 1536
TILE = 384
KT = 3
LAYERS = 8
TILES = 32
TOKENS = 12288


def draw_tile_lists(key, part):
    key = jax.random.fold_in(key, 11)
    own_tiles = jnp.arange(TILES, dtype=jnp.int32)
    signs = (jax.random.randint(key, (TILES, KT - 1), 0, 2, dtype=jnp.int32) * 2 - 1).astype(jnp.int32)
    first_try = own_tiles[:, None] + signs
    inside = jnp.logical_and(first_try >= 0, first_try < TILES)
    chosen = jnp.where(inside, first_try, own_tiles[:, None] - signs).astype(jnp.int32)
    return jnp.concatenate([own_tiles[:, None], chosen], axis=1).astype(jnp.int32)


def level_of(own_key, shape, pieces, low, high):
    gain = 1.0
    for dim, parts in pieces:
        steps = jax.random.uniform(jax.random.fold_in(jax.random.fold_in(own_key, 6), dim), (parts,), jnp.float32, low / len(pieces), high / len(pieces))
        gain = gain * jnp.repeat(jnp.exp(steps), shape[dim] // parts).reshape((-1,) + (1,) * (len(shape) - 1 - dim))
    return gain


def gaussian(key, shape, scale, limit, split=(), held_as=jnp.bfloat16):
    values = scale * jax.random.normal(key, shape, jnp.float32)
    if split:
        values = values * level_of(key, shape, split, -0.22, 0.18)
    return jnp.clip(values, -limit, limit).astype(held_as)


def setup_inputs(seed: int = 0) -> dict:
    key_of = jax.random.split(jax.random.key(seed), 10)
    return {
        "hidden": gaussian(key_of[0], (TOKENS, D), 1.0, 6.0, ((0, 32),)),
        "kv_cache": gaussian(key_of[1], (LAYERS, TOKENS, 2 * HD), 1.0, 6.0, ((0, 8), (1, 32))),
        "q_weight": gaussian(key_of[2], (LAYERS, D, HD), D ** -0.5, 0.109375, ((0, 8), (1, 32))),
        "o_weight": gaussian(key_of[3], (LAYERS, HD, D), HD ** -0.5, 0.15625, ((0, 8), (1, 32))),
        "mod_shift": gaussian(key_of[4], (LAYERS, D), 0.5, 3.0, ((0, 8),), jnp.float32),
        "mod_scale": gaussian(key_of[5], (LAYERS, D), 0.3, 1.5, ((0, 8),), jnp.float32),
        "mod_gate": jnp.clip(0.5 + 1.5 * jax.random.uniform(key_of[6], (LAYERS, D), jnp.float32) ** level_of(key_of[6], (LAYERS, D), ((0, 8),), -0.2, 0.2), 0.5, 2.0),
        "q_gain": jnp.clip(jnp.exp(math.log(6.0) - 2.4849066 * jax.random.uniform(key_of[7], (LAYERS, HEADS), jnp.float32) ** level_of(key_of[7], (LAYERS, HEADS), ((0, 8),), -0.2, 0.2)), 0.5, 6.0),
        "tile_lists": draw_tile_lists(jax.random.fold_in(key_of[9], 71), 0),
    }


epsilon = 1e-06

def unit_heads(values_in, head_count):
    split_rows = values_in.reshape(values_in.shape[0], head_count, -1)
    return split_rows * lax.rsqrt(lax.optimization_barrier(jnp.mean(split_rows * split_rows, axis=-1, keepdims=True)) + epsilon)

def reference(hidden, kv_cache, q_weight, o_weight, mod_shift, mod_scale, mod_gate, q_gain, tile_lists):
    current = hidden
    outputs = []
    for layer_index in range(LAYERS):
        state_f32 = current.astype(jnp.float32)
        row_mean = lax.optimization_barrier(jnp.mean(state_f32, axis=1, keepdims=True))
        centered = state_f32 - row_mean
        variance = lax.optimization_barrier(jnp.mean(centered * centered, axis=1, keepdims=True))
        normed = (centered * lax.rsqrt(variance + epsilon) * (1.0 + mod_scale[layer_index]) + mod_shift[layer_index]).astype(jnp.bfloat16)
        query = jnp.dot(normed, q_weight[layer_index], preferred_element_type=jnp.float32)
        query_unit = (unit_heads(query, HEADS) * (q_gain[layer_index][:, None] / math.sqrt(HDIM))).astype(jnp.bfloat16)
        cache_now = kv_cache[layer_index]
        key_unit = unit_heads(cache_now[:, :HD].astype(jnp.float32), HEADS).astype(jnp.bfloat16)
        key_tiles = key_unit.reshape(TILES, TILE, HEADS, HDIM)
        value_tiles = cache_now[:, HD:].reshape(TILES, TILE, HEADS, HDIM)
        query_tiles = query_unit.reshape(TILES, TILE, HEADS, HDIM)

        def one_tile(tile_args):
            q_tile, picked = tile_args
            key_rows = key_tiles[picked].reshape(KT * TILE, HEADS, HDIM).astype(jnp.float32)
            value_rows = value_tiles[picked].reshape(KT * TILE, HEADS, HDIM).astype(jnp.float32)
            scores = jnp.einsum('qhd,khd->hqk', q_tile.astype(jnp.float32), key_rows)
            raised = jnp.exp(scores)
            attn_probs = (raised / lax.optimization_barrier(jnp.sum(raised, axis=-1, keepdims=True))).astype(jnp.bfloat16)
            mixed = jnp.einsum('hqk,khd->qhd', attn_probs.astype(jnp.float32), value_rows)
            return mixed.astype(jnp.bfloat16)
        attended = lax.map(one_tile, (query_tiles, tile_lists)).reshape(TOKENS, HD)
        branch = jnp.dot(attended, o_weight[layer_index], preferred_element_type=jnp.float32)
        current = (state_f32 + mod_gate[layer_index] * branch).astype(jnp.bfloat16)
        outputs.append(current)
    return jnp.stack(outputs)
```

```python
import functools
import math

import jax
import jax.numpy as jnp
from jax import lax
from jax.experimental import pallas as pl
from jax.experimental.pallas import tpu as pltpu
from jax.sharding import PartitionSpec as P

TILE = 384
HEAD = 128
EPS = 1e-06
MIB = 2**20
F32 = jnp.float32
BF16 = jnp.bfloat16

ANY = pl.BlockSpec(memory_space=pl.ANY)
VMEM = pl.BlockSpec(memory_space=pltpu.VMEM)
SMEM = pl.BlockSpec(memory_space=pltpu.SMEM)

NY, NZ = 4, 8
BATCHES = 4
SKEW = 2
TOP = 16


def in_hbm(x):
    return pltpu.with_memory_space_constraint(x, pltpu.HBM)


def along_z(step):
    return [(y * NZ + z, y * NZ + (z + step) % NZ) for y in range(NY) for z in range(NZ)]


def along_y(step):
    return [(y * NZ + z, ((y + step) % NY) * NZ + z) for y in range(NY) for z in range(NZ)]


def ring(block, pairs, size):
    ahead = behind = block
    found = [block]
    for _ in range(1, size // 2):
        behind = lax.ppermute(behind, "seq", pairs(1))
        ahead = lax.ppermute(ahead, "seq", pairs(-1))
        found += [behind, ahead]
    half = block.shape[0] // 2
    found.append(lax.ppermute(behind[:half], "seq", pairs(1)))
    found.append(lax.ppermute(ahead[half:], "seq", pairs(-1)))
    return found


def offsets(size):
    out = [0]
    for k in range(1, size // 2):
        out += [-k, k]
    return out + [size // 2]


def keys_body(kv, out):
    width = kv.shape[1] // 2
    for c in range(0, width, HEAD):
        k = kv[:, c : c + HEAD].astype(F32)
        out[:, c : c + HEAD] = (k * lax.rsqrt(jnp.mean(k * k, axis=1, keepdims=True) + EPS)).astype(BF16)
    out[:, width:] = kv[:, width:]


def unit_keys(kv):
    return pl.pallas_call(
        keys_body,
        in_specs=[VMEM],
        out_specs=VMEM,
        out_shape=jax.ShapeDtypeStruct(kv.shape, BF16),
        compiler_params=pltpu.CompilerParams(vmem_limit_bytes=16 * MIB),
        name="unit_keys",
    )(kv)


def load_body(sizes, y_parts, z_parts, place, *refs):
    rows_q, rows_o = sizes
    n = len(y_parts) + len(z_parts)
    a_refs, b_refs = refs[: len(y_parts)], refs[len(y_parts) : n]
    kv_refs = refs[n : n + 3]
    wq, wo, kv, sems = refs[n + 3 :]
    width = wq.shape[1]
    y, z = place[0], place[1]
    copies = []

    def go(src, dst, group):
        c = pltpu.make_async_copy(src, dst, sems.at[group])
        c.start()
        copies.append(c)

    z_order = offsets(NZ)
    piece = rows_q + 2 * TOP
    for ref, (dy, lo) in zip(a_refs, y_parts):
        yy = lax.rem(y + dy + NY, NY)
        for k in range(ref.shape[0] // piece):
            zz = lax.rem(z + z_order[lo // piece + k] + NZ, NZ)
            s = yy * NZ + zz
            base = k * piece
            go(ref.at[pl.ds(base, rows_q)], wq.at[pl.ds(pl.multiple_of(s * rows_q, 16), rows_q)], 0)
            at = pl.ds(pl.multiple_of(s * rows_o, 16), TOP)
            go(ref.at[pl.ds(base + rows_q, TOP)], wo.at[at, pl.ds(0, width)], 1)
            go(ref.at[pl.ds(base + rows_q + TOP, TOP)], wo.at[at, pl.ds(width, width)], 1)
    y_order = offsets(NY)
    low = rows_o - TOP
    for ref, (dz, lo) in zip(b_refs, z_parts):
        zz = lax.rem(z + dz + NZ, NZ)
        for k in range(ref.shape[0] // low):
            yy = lax.rem(y + y_order[lo // low + k] + NY, NY)
            at = pl.ds(pl.multiple_of((yy * NZ + zz) * rows_o + TOP, 16), low)
            go(ref.at[pl.ds(k * low, low)], wo.at[at], 1)
    for i, ref in enumerate(kv_refs):
        go(ref, kv.at[pl.ds(i * TILE, TILE)], 2)
    for c in copies:
        c.wait()


def load(place, sizes, a_blocks, y_parts, b_blocks, z_parts, tiles, model, width):
    return pl.pallas_call(
        functools.partial(load_body, sizes, y_parts, z_parts),
        in_specs=[SMEM] + [ANY] * (len(a_blocks) + len(b_blocks) + 3),
        out_specs=[VMEM] * 3,
        out_shape=[
            pltpu.VMEM((model, width), BF16),
            pltpu.VMEM((width, model), BF16),
            pltpu.VMEM((3 * TILE, 2 * width), BF16),
        ],
        scratch_shapes=[pltpu.SemaphoreType.DMA((3,))],
        compiler_params=pltpu.CompilerParams(vmem_limit_bytes=4 * MIB),
        name="load",
    )(place, *[in_hbm(x) for x in (*a_blocks, *b_blocks, *tiles)])


def turn_body(
    turn, info, arrived, hidden, wq, wo, kv, scale, shift, gate, gain, mult, written_in, result, written,
    x_buf, n_buf, q_buf, a_buf, out_buf, in_sem, out_sems,
):
    rows, model = x_buf.shape
    width = wq.shape[1]
    section = info[2]
    micro = turn - SKEW * section

    @pl.when(jnp.logical_and(micro >= 0, micro < BATCHES))
    def _():
        row = pl.multiple_of(micro * rows, 16)

        @pl.when(section == 0)
        def _():
            c = pltpu.make_async_copy(hidden.at[pl.ds(row, rows)], x_buf, in_sem)
            c.start()
            c.wait()

        @pl.when(section != 0)
        def _():
            c = pltpu.make_async_copy(arrived, x_buf, in_sem)
            c.start()
            c.wait()

        x = x_buf[...].astype(F32)
        centered = x - jnp.mean(x, axis=1, keepdims=True)
        var = jnp.mean(centered * centered, axis=1, keepdims=True)
        n_buf[...] = (centered * lax.rsqrt(var + EPS) * (1.0 + scale[...]) + shift[...]).astype(BF16)
        step = width // 2
        for c in range(0, width, step):
            q_buf[:, c : c + step] = jnp.dot(n_buf[...], wq[:, c : c + step], preferred_element_type=F32)
        zero = jnp.zeros((rows, HEAD), BF16)

        def unit(c):
            q = q_buf[:, c : c + HEAD]
            r = lax.rsqrt(jnp.mean(q * q, axis=1, keepdims=True) + EPS)
            return (q * r * gain[:, c : c + HEAD]).astype(BF16)

        for c in range(0, width, 2 * HEAD):
            pair = jnp.concatenate(
                [
                    jnp.concatenate([unit(c), zero], axis=1),
                    jnp.concatenate([zero, unit(c + HEAD)], axis=1),
                ],
                axis=0,
            )
            s = lax.dot_general(
                pair, kv[:, c : c + 2 * HEAD], (((1,), (1,)), ((), ())), preferred_element_type=F32
            )
            e = jnp.exp(s) * mult[...]
            total = jnp.sum(e, axis=1, keepdims=True)
            mixed = jnp.dot(
                e.astype(BF16), kv[:, width + c : width + c + 2 * HEAD], preferred_element_type=F32
            )
            mixed = mixed / total
            a_buf[:, c : c + HEAD] = mixed[:rows, :HEAD].astype(BF16)
            a_buf[:, c + HEAD : c + 2 * HEAD] = mixed[rows:, HEAD:].astype(BF16)
        step = model // 4
        for c in range(0, model, step):
            branch = jnp.dot(a_buf[...], wo[:, c : c + step], preferred_element_type=F32)
            out_buf[:, c : c + step] = (
                x_buf[:, c : c + step].astype(F32) + gate[:, c : c + step] * branch
            ).astype(BF16)
        c1 = pltpu.make_async_copy(out_buf, result, out_sems.at[0])
        c2 = pltpu.make_async_copy(out_buf, written.at[pl.ds(row, rows)], out_sems.at[1])
        c1.start()
        c2.start()
        c1.wait()
        c2.wait()


def take_turn(turn, info, arrived, hidden, wq, wo, kv, scale, shift, gate, gain, mult, written):
    rows, model = arrived.shape
    width = wq.shape[1]
    keys = kv.shape[0]
    return pl.pallas_call(
        functools.partial(turn_body, turn),
        in_specs=[SMEM, ANY, ANY] + [VMEM] * 8 + [ANY],
        out_specs=[ANY, ANY],
        out_shape=[
            jax.ShapeDtypeStruct((rows, model), BF16),
            jax.ShapeDtypeStruct(written.shape, BF16),
        ],
        input_output_aliases={11: 1},
        scratch_shapes=[
            pltpu.VMEM((rows, model), BF16),
            pltpu.VMEM((rows, model), BF16),
            pltpu.VMEM((rows, width), F32),
            pltpu.VMEM((rows, width), BF16),
            pltpu.VMEM((rows, model), BF16),
            pltpu.SemaphoreType.DMA,
            pltpu.SemaphoreType.DMA((2,)),
        ],
        compiler_params=pltpu.CompilerParams(vmem_limit_bytes=20 * MIB),
        cost_estimate=pl.CostEstimate(
            flops=4 * rows * width * (model + keys),
            bytes_accessed=26 * MIB,
            transcendentals=rows * keys * (width // HEAD),
        ),
        name="turn",
    )(info, arrived, hidden, wq, wo, kv, scale, shift, gate, gain, mult, written)


def shards(
    hidden, kv_cache, q_weight, o_weight, mod_shift, mod_scale, mod_gate, q_gain, tile_lists
):
    tokens, model = hidden.shape
    heads = q_gain.shape[1]
    width = heads * HEAD
    rows_q, rows_o = q_weight.shape[1], o_weight.shape[1]
    section = lax.axis_index("segment")
    sections = lax.axis_size("segment")
    seq = lax.axis_index("seq")
    info = jnp.stack([seq // NZ, seq % NZ, section]).astype(jnp.int32)

    q_own, o_own = q_weight[0], o_weight[0]
    a_own = jnp.concatenate([q_own, o_own[:TOP, :width], o_own[:TOP, width:]], axis=0)
    b_own = o_own[TOP:]
    a_z = jnp.concatenate(ring(a_own, along_z, NZ), axis=0)
    b_y = jnp.concatenate(ring(b_own, along_y, NY), axis=0)
    own = unit_keys(kv_cache[0])
    left = lax.ppermute(own, "seq", [(i, i + 1) for i in range(NY * NZ - 1)])
    right = lax.ppermute(own, "seq", [(i + 1, i) for i in range(NY * NZ - 1)])
    a_blocks = ring(a_z, along_y, NY)
    b_blocks = ring(b_y, along_z, NZ)
    half_a, half_b = a_z.shape[0] // 2, b_y.shape[0] // 2
    y_parts = [(d, 0) for d in offsets(NY)] + [(NY // 2, half_a)]
    z_parts = [(d, 0) for d in offsets(NZ)] + [(NZ // 2, half_b)]
    wq, wo, kv = load(
        info, (rows_q, rows_o), a_blocks, y_parts, b_blocks, z_parts, (own, left, right), model, width
    )

    gain = jnp.repeat(q_gain / math.sqrt(HEAD), HEAD, axis=1)
    listed = [jnp.sum((tile_lists[0] == seq + d).astype(F32)) for d in (0, -1, 1)]
    mult = jnp.repeat(jnp.stack(listed)[None], TILE, axis=1)
    rows = tokens // BATCHES
    written = jnp.zeros((tokens, model), BF16)
    arrived = [hidden[:rows]] * SKEW
    for turn in range(SKEW * (sections - 1) + BATCHES):
        result, written = take_turn(
            turn, info, arrived[turn], hidden, wq, wo, kv, mod_scale, mod_shift, mod_gate, gain, mult, written
        )
        pairs = [(l, l + 1) for l in range(sections - 1) if 0 <= turn - SKEW * l < BATCHES]
        arrived.append(lax.ppermute(result, "segment", pairs) if pairs else result)
    return written[None]


def solution(mesh):
    placed = (
        P("seq", None),
        P("segment", "seq", None),
        P("segment", "seq", None),
        P("segment", "seq", None),
        P("segment", None),
        P("segment", None),
        P("segment", None),
        P("segment", None),
        P("seq", None),
    )
    return jax.shard_map(
        shards, mesh=mesh, in_specs=placed, out_specs=P("segment", "seq", None), check_vma=False
    )
```

```python
import functools
import math

import jax
import jax.numpy as jnp
from jax import lax
from jax.experimental import pallas as pl
from jax.experimental.pallas import tpu as pltpu
from jax.sharding import PartitionSpec as P

TILE = 384
HEAD = 128
EPS = 1e-06
MIB = 2**20
F32 = jnp.float32
BF16 = jnp.bfloat16

ANY = pl.BlockSpec(memory_space=pl.ANY)
VMEM = pl.BlockSpec(memory_space=pltpu.VMEM)
SMEM = pl.BlockSpec(memory_space=pltpu.SMEM)

NY, NZ = 4, 8
BATCHES = 4
OUT_PARTS = 2
SKEW = 2


def in_hbm(x):
    return pltpu.with_memory_space_constraint(x, pltpu.HBM)


def along_z(step):
    return [(y * NZ + z, y * NZ + (z + step) % NZ) for y in range(NY) for z in range(NZ)]


def along_y(step):
    return [(y * NZ + z, ((y + step) % NY) * NZ + z) for y in range(NY) for z in range(NZ)]


def ring(block, pairs, size, cut):
    ahead = behind = block
    found = [block]
    for _ in range(1, size // 2):
        behind = lax.ppermute(behind, "seq", pairs(1))
        ahead = lax.ppermute(ahead, "seq", pairs(-1))
        found += [behind, ahead]
    found.append(lax.ppermute(behind[:cut], "seq", pairs(1)))
    found.append(lax.ppermute(ahead[cut:], "seq", pairs(-1)))
    return found


def offsets(size):
    out = [0]
    for k in range(1, size // 2):
        out += [-k, k]
    return out + [size // 2]


def pieces(found):
    return found[:-2] + [jnp.concatenate(found[-2:], axis=0)]


A_PIECE = ((0, 96, "q", 0), (96, 16, "left", 0), (112, 16, "right", 0))
B_PIECE = ((0, 32, "left", 16), (32, 32, "right", 16))
A_ROWS, B_ROWS = 128, 64
A_CUT, B_CUT = 64, 32


def load_weights_body(plan, rows_q, rows_o, fresh, place, *refs):
    n = len(plan)
    blocks = refs[:n]
    wq, wo, *done, sem = refs[n if fresh else n + 2 :]
    width = wq.shape[1]
    y, z = place[0], place[1]
    copies = []
    for ref, found in zip(blocks, plan):
        for k, (dy, dz, piece, size) in enumerate(found):
            s = lax.rem(y + dy + NY, NY) * NZ + lax.rem(z + dz + NZ, NZ)
            for row, count, kind, at in piece:
                src = ref.at[pl.ds(k * size + row, count)]
                if kind == "q":
                    dst = wq.at[pl.ds(pl.multiple_of(s * rows_q + at, 16), count)]
                else:
                    here = pl.ds(pl.multiple_of(s * rows_o + at, 16), count)
                    dst = wo.at[here, pl.ds(0 if kind == "left" else width, width)]
                copies.append(pltpu.make_async_copy(src, dst, sem))
    for c in copies:
        c.start()
    for token in done:
        token[...] = jnp.zeros(token.shape, token.dtype)
    for c in copies:
        c.wait()


def load_weights(place, blocks, plan, rows_q, rows_o, model, width, held):
    fresh = held is None
    n = len(blocks)
    return pl.pallas_call(
        functools.partial(load_weights_body, plan, rows_q, rows_o, fresh),
        in_specs=[SMEM] + [ANY] * n + ([] if fresh else [VMEM] * 2),
        out_specs=[VMEM] * (3 if fresh else 2),
        out_shape=[pltpu.VMEM((model, width), BF16), pltpu.VMEM((width, model), BF16)]
        + [jax.ShapeDtypeStruct((8, 128), F32)] * fresh,
        input_output_aliases={} if fresh else {n + 1: 0, n + 2: 1},
        scratch_shapes=[pltpu.SemaphoreType.DMA],
        compiler_params=pltpu.CompilerParams(vmem_limit_bytes=4 * MIB),
        name="load_weights",
    )(place, *[in_hbm(x) for x in blocks], *([] if fresh else held))


def load_tiles_body(place, own, before, before_low, after, after_low, kv, sems):
    z, half = place[1], TILE // 2

    def copy(src, at, k):
        return pltpu.make_async_copy(src, kv.at[pl.ds(at, src.shape[0])], sems.at[k])

    def pick(edge, low, tile, at, k):
        @pl.when(z == edge)
        def _():
            copy(low, at, k).start()

        @pl.when(z != edge)
        def _():
            copy(tile.at[pl.ds(half, half)], at, k).start()

    copies = [
        [copy(own, 0, 0)],
        [copy(before.at[pl.ds(0, half)], TILE, 1), copy(before_low, TILE + half, 2)],
        [copy(after.at[pl.ds(0, half)], 2 * TILE, 3), copy(after_low, 2 * TILE + half, 4)],
    ]
    for group in copies:
        group[0].start()
    pick(0, before_low, before, TILE + half, 2)
    pick(NZ - 1, after_low, after, 2 * TILE + half, 4)
    width = kv.shape[1] // 2
    for i, group in enumerate(copies):
        for c in group:
            c.wait()
        rows = slice(i * TILE, (i + 1) * TILE)
        for c in range(0, width, HEAD):
            k = kv[rows, c : c + HEAD].astype(F32)
            r = lax.rsqrt(jnp.mean(k * k, axis=1, keepdims=True) + EPS)
            kv[rows, c : c + HEAD] = (k * r).astype(BF16)


def load_tiles(place, *tiles):
    return pl.pallas_call(
        load_tiles_body,
        in_specs=[SMEM] + [ANY] * 5,
        out_specs=VMEM,
        out_shape=pltpu.VMEM((3 * TILE, tiles[0].shape[1]), BF16),
        scratch_shapes=[pltpu.SemaphoreType.DMA((5,))],
        compiler_params=pltpu.CompilerParams(vmem_limit_bytes=8 * MIB),
        name="load_tiles",
    )(place, *[in_hbm(x) for x in tiles])


def turn_body(
    turn, info, arrived, hidden, wq, wo, kv, scale, shift, gate, gain, mult, *refs
):
    result, written, x_buf, n_buf, q_buf, a_buf, out_buf, in_sem, out_sems = refs[-9:]
    rows, model = x_buf.shape
    width = wq.shape[1]
    section = info[2]
    micro = turn - SKEW * section

    @pl.when(jnp.logical_and(micro >= 0, micro < BATCHES))
    def _():
        row = pl.multiple_of(micro * rows, 16)

        @pl.when(section == 0)
        def _():
            c = pltpu.make_async_copy(hidden.at[pl.ds(row, rows)], x_buf, in_sem)
            c.start()
            c.wait()

        @pl.when(section != 0)
        def _():
            c = pltpu.make_async_copy(arrived.at[pl.ds(0, rows)], x_buf, in_sem)
            c.start()
            c.wait()

        x = x_buf[...].astype(F32)
        centered = x - jnp.mean(x, axis=1, keepdims=True)
        var = jnp.mean(centered * centered, axis=1, keepdims=True)
        n_buf[...] = (centered * lax.rsqrt(var + EPS) * (1.0 + scale[...]) + shift[...]).astype(BF16)
        zero = jnp.zeros((rows, HEAD), BF16)
        two = 2 * HEAD

        def project(c):
            q_buf[:, c : c + two] = jnp.dot(n_buf[...], wq[:, c : c + two], preferred_element_type=F32)

        def unit(c):
            q = q_buf[:, c : c + HEAD]
            r = lax.rsqrt(jnp.mean(q * q, axis=1, keepdims=True) + EPS)
            return (q * r * gain[:, c : c + HEAD]).astype(BF16)

        def score(c):
            pair = jnp.concatenate(
                [
                    jnp.concatenate([unit(c), zero], axis=1),
                    jnp.concatenate([zero, unit(c + HEAD)], axis=1),
                ],
                axis=0,
            )
            return lax.dot_general(
                pair, kv[:, c : c + two], (((1,), (1,)), ((), ())), preferred_element_type=F32
            )

        def mix(c, s):
            e = jnp.exp(s) * mult[...]
            share = 1.0 / jnp.sum(e, axis=1, keepdims=True)
            mixed = jnp.dot(
                e.astype(BF16), kv[:, width + c : width + c + two], preferred_element_type=F32
            )
            a_buf[:, c : c + HEAD] = (mixed[:rows, :HEAD] * share[:rows]).astype(BF16)
            a_buf[:, c + HEAD : c + two] = (mixed[rows:, HEAD:] * share[rows:]).astype(BF16)

        starts = list(range(0, width, two))
        project(starts[0])
        project(starts[1])
        ahead = score(starts[0])
        for i, c in enumerate(starts):
            now = ahead
            if i + 2 < len(starts):
                project(starts[i + 2])
            if i + 1 < len(starts):
                ahead = score(starts[i + 1])
            mix(c, now)
        step = model // OUT_PARTS
        copies = []
        for i, c in enumerate(range(0, model, step)):
            here = pl.ds(c, step)
            branch = jnp.dot(a_buf[...], wo[:, c : c + step], preferred_element_type=F32)
            out_buf[:, c : c + step] = (
                x_buf[:, c : c + step].astype(F32) + gate[:, c : c + step] * branch
            ).astype(BF16)
            for k, dst in enumerate((result.at[:, here], written.at[pl.ds(row, rows), here])):
                copies.append(pltpu.make_async_copy(out_buf.at[:, here], dst, out_sems.at[2 * i + k]))
                copies[-1].start()
        for c in copies:
            c.wait()


def take_turn(turn, info, arrived, hidden, wq, wo, kv, scale, shift, gate, gain, mult, written):
    tokens, model = hidden.shape
    rows = tokens // BATCHES
    width = wq.shape[1]
    keys = kv.shape[0]
    return pl.pallas_call(
        functools.partial(turn_body, turn),
        in_specs=[SMEM, ANY, ANY] + [VMEM] * 8 + [ANY] * len(written),
        out_specs=[ANY, ANY],
        out_shape=[
            jax.ShapeDtypeStruct((rows, model), BF16),
            jax.ShapeDtypeStruct(hidden.shape, BF16),
        ],
        input_output_aliases={11: 1} if written else {},
        scratch_shapes=[
            pltpu.VMEM((rows, model), BF16),
            pltpu.VMEM((rows, model), BF16),
            pltpu.VMEM((rows, width), F32),
            pltpu.VMEM((rows, width), BF16),
            pltpu.VMEM((rows, model), BF16),
            pltpu.SemaphoreType.DMA,
            pltpu.SemaphoreType.DMA((2 * OUT_PARTS,)),
        ],
        compiler_params=pltpu.CompilerParams(vmem_limit_bytes=12 * MIB),
        cost_estimate=pl.CostEstimate(
            flops=4 * rows * width * (model + keys),
            bytes_accessed=26 * MIB,
            transcendentals=rows * keys * (width // HEAD),
        ),
        name="turn",
    )(info, arrived, hidden, wq, wo, kv, scale, shift, gate, gain, mult, *written)


def shards(
    hidden, kv_cache, q_weight, o_weight, mod_shift, mod_scale, mod_gate, q_gain, tile_lists
):
    tokens, model = hidden.shape
    heads = q_gain.shape[1]
    width = heads * HEAD
    rows_q, rows_o = q_weight.shape[1], o_weight.shape[1]
    section = lax.axis_index("segment")
    sections = lax.axis_size("segment")
    seq = lax.axis_index("seq")
    info = jnp.stack([seq // NZ, seq % NZ, section]).astype(jnp.int32)

    own = kv_cache[0]
    z_order, y_order = offsets(NZ), offsets(NY)
    q_own, o_own = q_weight[0], o_weight[0]

    def shard_piece(piece):
        cut = {"q": (q_own, 0), "left": (o_own, 0), "right": (o_own, width)}
        return jnp.concatenate(
            [
                cut[kind][0][at : at + count, cut[kind][1] : cut[kind][1] + width]
                for _, count, kind, at in piece
            ],
            axis=0,
        )

    def send(x, pairs):
        return lax.ppermute(x, "seq", pairs)

    a_z = jnp.concatenate(pieces(ring(shard_piece(A_PIECE), along_z, NZ, A_CUT)), axis=0)
    b_y = jnp.concatenate(pieces(ring(shard_piece(B_PIECE), along_y, NY, B_CUT)), axis=0)
    half = tokens // 2
    edge, b_y = lax.optimization_barrier((own[:half], b_y))
    crossed_up = send(edge, [(y * NZ + NZ - 1, (y + 1) * NZ + NZ - 1) for y in range(NY - 1)])
    crossed_down = send(edge, [((y + 1) * NZ, y * NZ) for y in range(NY - 1)])
    z_here = seq % NZ
    up = jnp.concatenate([jnp.where(z_here == NZ - 1, crossed_up, own[:half]), own[half:]], axis=0)
    down = jnp.concatenate([jnp.where(z_here == 0, crossed_down, own[:half]), own[half:]], axis=0)
    a_z, b_y, up, down = lax.optimization_barrier((a_z, b_y, up, down))
    a_behind, a_ahead = send(a_z, along_y(1)), send(a_z, along_y(-1))
    before, after = send(up, along_z(1)), send(down, along_z(-1))
    b_y, before, after, low_b, low_a = lax.optimization_barrier((b_y, before, after, before[half:], after[half:]))
    before_low = send(low_b, [(y * NZ, (y + 1) * NZ) for y in range(NY - 1)])
    after_low = send(low_a, [((y + 1) * NZ + NZ - 1, y * NZ + NZ - 1) for y in range(NY - 1)])
    b1 = [send(b_y, along_z(1)), send(b_y, along_z(-1))]
    half_a, half_b = a_z.shape[0] // 2, b_y.shape[0] // 2
    quarter = half_a // 2
    parts = (
        a_behind[:quarter], a_ahead[half_a : half_a + quarter],
        a_behind[quarter:half_a], a_ahead[half_a + quarter :],
    )
    *b1, low, high, low2, high2 = lax.optimization_barrier((*b1, *parts))
    a_last = [send(low, along_y(1)), send(high, along_y(-1))]
    *a_last, low2, high2 = lax.optimization_barrier((*a_last, low2, high2))
    a_last += [send(low2, along_y(1)), send(high2, along_y(-1))]
    b2 = [send(b1[0], along_z(1)), send(b1[1], along_z(-1))]

    def a_plan(dy, order):
        return [(dy, dz, A_PIECE, A_ROWS) for dz in order]

    def b_plan(dz, order):
        return [(dy, dz, B_PIECE, B_ROWS) for dy in order]

    sizes = (rows_q, rows_o, model, width)
    few_z, few_y = NZ // 2, NY // 2
    plan = [*[a_plan(d, z_order) for d in (0, -1, 1)], *[b_plan(d, y_order) for d in (0, -1, 1)]]
    *held, token = load_weights(info, [a_z, a_behind, a_ahead, b_y, *b1], plan, *sizes, None)
    *b2, token = lax.optimization_barrier((*b2, token))
    b3 = [send(b2[0], along_z(1)), send(b2[1], along_z(-1))]
    b_last = [send(b3[0][:half_b], along_z(1)), send(b3[1][half_b:], along_z(-1))]
    kv = load_tiles(info, own, before, before_low, after, after_low)
    held = load_weights(info, [*b2], [b_plan(d, y_order) for d in (-2, 2)], *sizes, held)
    plan = [
        *[b_plan(d, y_order) for d in (-3, 3)],
        *[a_plan(few_y, z_order[k : k + 2]) for k in (0, few_z, 2, few_z + 2)],
        b_plan(few_z, y_order[:few_y]),
        b_plan(few_z, y_order[few_y:]),
    ]
    wq, wo = load_weights(info, [*b3, *a_last, *b_last], plan, *sizes, held)

    gain = jnp.repeat(q_gain / math.sqrt(HEAD), HEAD, axis=1)
    listed = [jnp.sum((tile_lists[0] == seq + d).astype(F32)) for d in (0, -1, 1)]
    mult = jnp.repeat(jnp.stack(listed)[None], TILE, axis=1)
    written = []
    arrived = [hidden] * SKEW
    for turn in range(SKEW * (sections - 1) + BATCHES):
        result, *written = take_turn(
            turn, info, arrived[turn], hidden, wq, wo, kv, mod_scale, mod_shift, mod_gate, gain, mult, written
        )
        pairs = [(l, l + 1) for l in range(sections - 1) if 0 <= turn - SKEW * l < BATCHES]
        arrived.append(lax.ppermute(result, "segment", pairs) if pairs else result)
    return written[0][None]


def solution(mesh):
    placed = (
        P("seq", None),
        P("segment", "seq", None),
        P("segment", "seq", None),
        P("segment", "seq", None),
        P("segment", None),
        P("segment", None),
        P("segment", None),
        P("segment", None),
        P("seq", None),
    )
    return jax.shard_map(
        shards, mesh=mesh, in_specs=placed, out_specs=P("segment", "seq", None), check_vma=False
    )
```

```python
import functools
import math

import jax
import jax.numpy as jnp
from jax import lax
from jax.experimental import pallas as pl
from jax.experimental.pallas import tpu as pltpu
from jax.sharding import PartitionSpec as P

TILE = 384
HEAD = 128
EPS = 1e-06
MIB = 2**20
F32 = jnp.float32
BF16 = jnp.bfloat16

ANY = pl.BlockSpec(memory_space=pl.ANY)
VMEM = pl.BlockSpec(memory_space=pltpu.VMEM)
SMEM = pl.BlockSpec(memory_space=pltpu.SMEM)

NY, NZ = 4, 8
BATCHES = 4
OUT_PARTS = 2
SKEW = 2


def in_hbm(x):
    return pltpu.with_memory_space_constraint(x, pltpu.HBM)


def along_z(step):
    return [(y * NZ + z, y * NZ + (z + step) % NZ) for y in range(NY) for z in range(NZ)]


def along_y(step):
    return [(y * NZ + z, ((y + step) % NY) * NZ + z) for y in range(NY) for z in range(NZ)]


def ring(block, pairs, size, cut):
    ahead = behind = block
    found = [block]
    for _ in range(1, size // 2):
        behind = lax.ppermute(behind, "seq", pairs(1))
        ahead = lax.ppermute(ahead, "seq", pairs(-1))
        found += [behind, ahead]
    found.append(lax.ppermute(behind[:cut], "seq", pairs(1)))
    found.append(lax.ppermute(ahead[cut:], "seq", pairs(-1)))
    return found


def offsets(size):
    out = [0]
    for k in range(1, size // 2):
        out += [-k, k]
    return out + [size // 2]


def pieces(found):
    return found[:-2] + [jnp.concatenate(found[-2:], axis=0)]


A_PIECE = ((0, 96, "q", 0), (96, 16, "left", 0), (112, 16, "right", 0))
B_PIECE = ((0, 32, "left", 16), (32, 32, "right", 16))
A_ROWS, B_ROWS = 128, 64
A_CUT, B_CUT = 64, 32


def load_weights_body(plan, rows_q, rows_o, fresh, place, *refs):
    n = len(plan)
    blocks = refs[:n]
    wq, wo, *done, sem = refs[n if fresh else n + 2 :]
    width = wq.shape[1]
    y, z = place[0], place[1]
    copies = []
    for ref, found in zip(blocks, plan):
        for k, (dy, dz, piece, size) in enumerate(found):
            s = lax.rem(y + dy + NY, NY) * NZ + lax.rem(z + dz + NZ, NZ)
            for row, count, kind, at in piece:
                src = ref.at[pl.ds(k * size + row, count)]
                if kind == "q":
                    dst = wq.at[pl.ds(pl.multiple_of(s * rows_q + at, 16), count)]
                else:
                    here = pl.ds(pl.multiple_of(s * rows_o + at, 16), count)
                    dst = wo.at[here, pl.ds(0 if kind == "left" else width, width)]
                copies.append(pltpu.make_async_copy(src, dst, sem))
    for c in copies:
        c.start()
    for token in done:
        token[...] = jnp.zeros(token.shape, token.dtype)
    for c in copies:
        c.wait()


def load_weights(place, blocks, plan, rows_q, rows_o, model, width, held):
    fresh = held is None
    n = len(blocks)
    return pl.pallas_call(
        functools.partial(load_weights_body, plan, rows_q, rows_o, fresh),
        in_specs=[SMEM] + [ANY] * n + ([] if fresh else [VMEM] * 2),
        out_specs=[VMEM] * (3 if fresh else 2),
        out_shape=[pltpu.VMEM((model, width), BF16), pltpu.VMEM((width, model), BF16)]
        + [jax.ShapeDtypeStruct((8, 128), F32)] * fresh,
        input_output_aliases={} if fresh else {n + 1: 0, n + 2: 1},
        scratch_shapes=[pltpu.SemaphoreType.DMA],
        compiler_params=pltpu.CompilerParams(vmem_limit_bytes=4 * MIB),
        name="load_weights",
    )(place, *[in_hbm(x) for x in blocks], *([] if fresh else held))


def hand_on_body(*refs):
    del refs


def hand_on(arrays, after):
    n = len(arrays)
    return pl.pallas_call(
        hand_on_body,
        in_specs=[ANY] * (n + 1),
        out_specs=[ANY] * n,
        out_shape=[jax.ShapeDtypeStruct(x.shape, x.dtype) for x in arrays],
        input_output_aliases={i: i for i in range(n)},
        compiler_params=pltpu.CompilerParams(vmem_limit_bytes=4 * MIB),
        name="hand_on",
    )(*arrays, after)


def normalise(kv, at, count):
    width = kv.shape[1] // 2
    rows = slice(at, at + count)
    for c in range(0, width, HEAD):
        k = kv[rows, c : c + HEAD].astype(F32)
        r = lax.rsqrt(jnp.mean(k * k, axis=1, keepdims=True) + EPS)
        kv[rows, c : c + HEAD] = (k * r).astype(BF16)


def load_tiles_body(own, before, after, kv, done, sems):
    half = TILE // 2
    places = ((own, 0), (before.at[pl.ds(0, half)], TILE), (after.at[pl.ds(0, half)], 2 * TILE))
    copies = [
        pltpu.make_async_copy(src, kv.at[pl.ds(at, src.shape[0])], sems.at[k])
        for k, (src, at) in enumerate(places)
    ]
    for c in copies:
        c.start()
    done[...] = jnp.zeros(done.shape, done.dtype)
    for c, (src, at) in zip(copies, places):
        c.wait()
        normalise(kv, at, src.shape[0])


def load_low_body(place, before, before_low, after, after_low, held, kv, sems):
    del held
    z, half = place[1], TILE // 2

    def copy(src, at, k):
        return pltpu.make_async_copy(src, kv.at[pl.ds(at, half)], sems.at[k])

    def pick(edge, low, tile, at, k):
        @pl.when(z == edge)
        def _():
            copy(low, at, k).start()

        @pl.when(z != edge)
        def _():
            copy(tile.at[pl.ds(half, half)], at, k).start()

    pick(0, before_low, before, TILE + half, 0)
    pick(NZ - 1, after_low, after, 2 * TILE + half, 1)
    for k, (low, at) in enumerate(((before_low, TILE + half), (after_low, 2 * TILE + half))):
        copy(low, at, k).wait()
        normalise(kv, at, half)


def load_tiles(*tiles):
    return pl.pallas_call(
        load_tiles_body,
        in_specs=[ANY] * 3,
        out_specs=[VMEM] * 2,
        out_shape=[
            pltpu.VMEM((3 * TILE, tiles[0].shape[1]), BF16),
            jax.ShapeDtypeStruct((8, 128), F32),
        ],
        scratch_shapes=[pltpu.SemaphoreType.DMA((3,))],
        compiler_params=pltpu.CompilerParams(vmem_limit_bytes=8 * MIB),
        name="load_tiles",
    )(*[in_hbm(x) for x in tiles])


def load_low(place, tiles, kv):
    return pl.pallas_call(
        load_low_body,
        in_specs=[SMEM] + [ANY] * 4 + [VMEM],
        out_specs=VMEM,
        out_shape=pltpu.VMEM(kv.shape, BF16),
        input_output_aliases={5: 0},
        scratch_shapes=[pltpu.SemaphoreType.DMA((2,))],
        compiler_params=pltpu.CompilerParams(vmem_limit_bytes=8 * MIB),
        name="load_low",
    )(place, *[in_hbm(x) for x in tiles], kv)


def turn_body(
    turn, info, arrived, hidden, wq, wo, kv, scale, shift, gate, gain, mult, *refs
):
    result, written, x_buf, n_buf, q_buf, a_buf, out_buf, in_sem, out_sems = refs[-9:]
    rows, model = x_buf.shape
    width = wq.shape[1]
    section = info[2]
    micro = turn - SKEW * section

    @pl.when(jnp.logical_and(micro >= 0, micro < BATCHES))
    def _():
        row = pl.multiple_of(micro * rows, 16)

        @pl.when(section == 0)
        def _():
            c = pltpu.make_async_copy(hidden.at[pl.ds(row, rows)], x_buf, in_sem)
            c.start()
            c.wait()

        @pl.when(section != 0)
        def _():
            c = pltpu.make_async_copy(arrived.at[pl.ds(0, rows)], x_buf, in_sem)
            c.start()
            c.wait()

        x = x_buf[...].astype(F32)
        centered = x - jnp.mean(x, axis=1, keepdims=True)
        var = jnp.mean(centered * centered, axis=1, keepdims=True)
        n_buf[...] = (centered * lax.rsqrt(var + EPS) * (1.0 + scale[...]) + shift[...]).astype(BF16)
        zero = jnp.zeros((rows, HEAD), BF16)
        two = 2 * HEAD

        def project(c):
            q_buf[:, c : c + two] = jnp.dot(n_buf[...], wq[:, c : c + two], preferred_element_type=F32)

        def unit(c):
            q = q_buf[:, c : c + HEAD]
            r = lax.rsqrt(jnp.mean(q * q, axis=1, keepdims=True) + EPS)
            return (q * r * gain[:, c : c + HEAD]).astype(BF16)

        def score(c):
            pair = jnp.concatenate(
                [
                    jnp.concatenate([unit(c), zero], axis=1),
                    jnp.concatenate([zero, unit(c + HEAD)], axis=1),
                ],
                axis=0,
            )
            return lax.dot_general(
                pair, kv[:, c : c + two], (((1,), (1,)), ((), ())), preferred_element_type=F32
            )

        def mix(c, s):
            e = jnp.exp(s) * mult[...]
            share = 1.0 / jnp.sum(e, axis=1, keepdims=True)
            mixed = jnp.dot(
                e.astype(BF16), kv[:, width + c : width + c + two], preferred_element_type=F32
            )
            a_buf[:, c : c + HEAD] = (mixed[:rows, :HEAD] * share[:rows]).astype(BF16)
            a_buf[:, c + HEAD : c + two] = (mixed[rows:, HEAD:] * share[rows:]).astype(BF16)

        starts = list(range(0, width, two))
        project(starts[0])
        project(starts[1])
        ahead = score(starts[0])
        for i, c in enumerate(starts):
            now = ahead
            if i + 2 < len(starts):
                project(starts[i + 2])
            if i + 1 < len(starts):
                ahead = score(starts[i + 1])
            mix(c, now)
        step = model // OUT_PARTS
        copies = []
        for i, c in enumerate(range(0, model, step)):
            here = pl.ds(c, step)
            branch = jnp.dot(a_buf[...], wo[:, c : c + step], preferred_element_type=F32)
            out_buf[:, c : c + step] = (
                x_buf[:, c : c + step].astype(F32) + gate[:, c : c + step] * branch
            ).astype(BF16)
            for k, dst in enumerate((result.at[:, here], written.at[pl.ds(row, rows), here])):
                copies.append(pltpu.make_async_copy(out_buf.at[:, here], dst, out_sems.at[2 * i + k]))
                copies[-1].start()
        for c in copies:
            c.wait()


def take_turn(turn, info, arrived, hidden, wq, wo, kv, scale, shift, gate, gain, mult, written):
    tokens, model = hidden.shape
    rows = tokens // BATCHES
    width = wq.shape[1]
    keys = kv.shape[0]
    return pl.pallas_call(
        functools.partial(turn_body, turn),
        in_specs=[SMEM, ANY, ANY] + [VMEM] * 8 + [ANY] * len(written),
        out_specs=[ANY, ANY],
        out_shape=[
            jax.ShapeDtypeStruct((rows, model), BF16),
            jax.ShapeDtypeStruct(hidden.shape, BF16),
        ],
        input_output_aliases={11: 1} if written else {},
        scratch_shapes=[
            pltpu.VMEM((rows, model), BF16),
            pltpu.VMEM((rows, model), BF16),
            pltpu.VMEM((rows, width), F32),
            pltpu.VMEM((rows, width), BF16),
            pltpu.VMEM((rows, model), BF16),
            pltpu.SemaphoreType.DMA,
            pltpu.SemaphoreType.DMA((2 * OUT_PARTS,)),
        ],
        compiler_params=pltpu.CompilerParams(vmem_limit_bytes=12 * MIB),
        cost_estimate=pl.CostEstimate(
            flops=4 * rows * width * (model + keys),
            bytes_accessed=26 * MIB,
            transcendentals=rows * keys * (width // HEAD),
        ),
        name="turn",
    )(info, arrived, hidden, wq, wo, kv, scale, shift, gate, gain, mult, *written)


def shards(
    hidden, kv_cache, q_weight, o_weight, mod_shift, mod_scale, mod_gate, q_gain, tile_lists
):
    tokens, model = hidden.shape
    heads = q_gain.shape[1]
    width = heads * HEAD
    rows_q, rows_o = q_weight.shape[1], o_weight.shape[1]
    section = lax.axis_index("segment")
    sections = lax.axis_size("segment")
    seq = lax.axis_index("seq")
    info = jnp.stack([seq // NZ, seq % NZ, section]).astype(jnp.int32)

    own = kv_cache[0]
    z_order, y_order = offsets(NZ), offsets(NY)
    q_own, o_own = q_weight[0], o_weight[0]

    def shard_piece(piece):
        cut = {"q": (q_own, 0), "left": (o_own, 0), "right": (o_own, width)}
        return jnp.concatenate(
            [
                cut[kind][0][at : at + count, cut[kind][1] : cut[kind][1] + width]
                for _, count, kind, at in piece
            ],
            axis=0,
        )

    def send(x, pairs):
        return lax.ppermute(x, "seq", pairs)

    a_z = jnp.concatenate(pieces(ring(shard_piece(A_PIECE), along_z, NZ, A_CUT)), axis=0)
    b_y = jnp.concatenate(pieces(ring(shard_piece(B_PIECE), along_y, NY, B_CUT)), axis=0)
    half = tokens // 2
    edge, b_y = lax.optimization_barrier((own[:half], b_y))
    crossed_up = send(edge, [(y * NZ + NZ - 1, (y + 1) * NZ + NZ - 1) for y in range(NY - 1)])
    crossed_down = send(edge, [((y + 1) * NZ, y * NZ) for y in range(NY - 1)])
    z_here = seq % NZ
    up = jnp.concatenate([jnp.where(z_here == NZ - 1, crossed_up, own[:half]), own[half:]], axis=0)
    down = jnp.concatenate([jnp.where(z_here == 0, crossed_down, own[:half]), own[half:]], axis=0)
    a_z, b_y, up, down = lax.optimization_barrier((a_z, b_y, up, down))
    a_behind, a_ahead = send(a_z, along_y(1)), send(a_z, along_y(-1))
    before, after = send(up, along_z(1)), send(down, along_z(-1))
    b_y, before, after, low_b, low_a = lax.optimization_barrier((b_y, before, after, before[half:], after[half:]))
    before_low = send(low_b, [(y * NZ, (y + 1) * NZ) for y in range(NY - 1)])
    after_low = send(low_a, [((y + 1) * NZ + NZ - 1, y * NZ + NZ - 1) for y in range(NY - 1)])
    b1 = [send(b_y, along_z(1)), send(b_y, along_z(-1))]
    half_a, half_b = a_z.shape[0] // 2, b_y.shape[0] // 2
    quarter = half_a // 2
    parts = (
        a_behind[:quarter], a_ahead[half_a : half_a + quarter],
        a_behind[quarter:half_a], a_ahead[half_a + quarter :],
    )
    *b1, low, high, low2, high2 = lax.optimization_barrier((*b1, *parts))
    a_last = [send(low, along_y(1)), send(high, along_y(-1))]
    *a_last, low2, high2 = lax.optimization_barrier((*a_last, low2, high2))
    a_last += [send(low2, along_y(1)), send(high2, along_y(-1))]
    b2 = [send(b1[0], along_z(1)), send(b1[1], along_z(-1))]

    def a_plan(dy, order):
        return [(dy, dz, A_PIECE, A_ROWS) for dz in order]

    def b_plan(dz, order):
        return [(dy, dz, B_PIECE, B_ROWS) for dy in order]

    sizes = (rows_q, rows_o, model, width)
    few_z, few_y = NZ // 2, NY // 2
    plan = [*[a_plan(d, z_order) for d in (0, -1, 1)], *[b_plan(d, y_order) for d in (0, -1, 1)]]
    *held, token = load_weights(info, [a_z, a_behind, a_ahead, b_y, *b1], plan, *sizes, None)
    b2 = hand_on(b2, token)
    b3 = [send(b2[0], along_z(1)), send(b2[1], along_z(-1))]
    kv, token = load_tiles(own, before, after)
    b3 = hand_on(b3, token)
    b_last = [send(b3[0][:half_b], along_z(1)), send(b3[1][half_b:], along_z(-1))]
    kv = load_low(info, (before, before_low, after, after_low), kv)
    held = load_weights(info, [*b2], [b_plan(d, y_order) for d in (-2, 2)], *sizes, held)
    plan = [
        *[b_plan(d, y_order) for d in (-3, 3)],
        *[a_plan(few_y, z_order[k : k + 2]) for k in (0, few_z, 2, few_z + 2)],
        b_plan(few_z, y_order[:few_y]),
        b_plan(few_z, y_order[few_y:]),
    ]
    wq, wo = load_weights(info, [*b3, *a_last, *b_last], plan, *sizes, held)

    gain = jnp.repeat(q_gain / math.sqrt(HEAD), HEAD, axis=1)
    listed = [jnp.sum((tile_lists[0] == seq + d).astype(F32)) for d in (0, -1, 1)]
    mult = jnp.repeat(jnp.stack(listed)[None], TILE, axis=1)
    written = []
    arrived = [hidden] * SKEW
    for turn in range(SKEW * (sections - 1) + BATCHES):
        result, *written = take_turn(
            turn, info, arrived[turn], hidden, wq, wo, kv, mod_scale, mod_shift, mod_gate, gain, mult, written
        )
        pairs = [(l, l + 1) for l in range(sections - 1) if 0 <= turn - SKEW * l < BATCHES]
        arrived.append(lax.ppermute(result, "segment", pairs) if pairs else result)
    return written[0][None]


def solution(mesh):
    placed = (
        P("seq", None),
        P("segment", "seq", None),
        P("segment", "seq", None),
        P("segment", "seq", None),
        P("segment", None),
        P("segment", None),
        P("segment", None),
        P("segment", None),
        P("seq", None),
    )
    return jax.shard_map(
        shards, mesh=mesh, in_specs=placed, out_specs=P("segment", "seq", None), check_vma=False
    )
```

```python
import functools
import math

import jax
import jax.numpy as jnp
from jax import lax
from jax.experimental import pallas as pl
from jax.experimental.pallas import tpu as pltpu
from jax.sharding import PartitionSpec as P

TILE = 384
HEAD = 128
EPS = 1e-06
MIB = 2**20
F32 = jnp.float32
BF16 = jnp.bfloat16

ANY = pl.BlockSpec(memory_space=pl.ANY)
VMEM = pl.BlockSpec(memory_space=pltpu.VMEM)
SMEM = pl.BlockSpec(memory_space=pltpu.SMEM)

NY, NZ = 4, 8
BATCHES = 4
OUT_PARTS = 2
SKEW = 2


def in_hbm(x):
    return pltpu.with_memory_space_constraint(x, pltpu.HBM)


def along_z(step):
    return [(y * NZ + z, y * NZ + (z + step) % NZ) for y in range(NY) for z in range(NZ)]


def along_y(step):
    return [(y * NZ + z, ((y + step) % NY) * NZ + z) for y in range(NY) for z in range(NZ)]


def ring(block, pairs, size, cut):
    ahead = behind = block
    found = [block]
    for _ in range(1, size // 2):
        behind = lax.ppermute(behind, "seq", pairs(1))
        ahead = lax.ppermute(ahead, "seq", pairs(-1))
        found += [behind, ahead]
    found.append(lax.ppermute(behind[:cut], "seq", pairs(1)))
    found.append(lax.ppermute(ahead[cut:], "seq", pairs(-1)))
    return found


def offsets(size):
    out = [0]
    for k in range(1, size // 2):
        out += [-k, k]
    return out + [size // 2]


def pieces(found):
    return found[:-2] + [jnp.concatenate(found[-2:], axis=0)]


A_PIECE = ((0, 96, "q", 0), (96, 16, "left", 0), (112, 16, "right", 0))
B_PIECE = ((0, 32, "left", 16), (32, 32, "right", 16))
A_ROWS, B_ROWS = 128, 64
A_CUT, B_CUT = 64, 32


def load_weights_body(plan, rows_q, rows_o, fresh, place, *refs):
    n = len(plan)
    blocks = refs[:n]
    wq, wo, *done, sem = refs[n if fresh else n + 2 :]
    width = wq.shape[1]
    y, z = place[0], place[1]
    copies = []
    for ref, found in zip(blocks, plan):
        for k, (dy, dz, piece, size) in enumerate(found):
            s = lax.rem(y + dy + NY, NY) * NZ + lax.rem(z + dz + NZ, NZ)
            for row, count, kind, at in piece:
                src = ref.at[pl.ds(k * size + row, count)]
                if kind == "q":
                    dst = wq.at[pl.ds(pl.multiple_of(s * rows_q + at, 16), count)]
                else:
                    here = pl.ds(pl.multiple_of(s * rows_o + at, 16), count)
                    dst = wo.at[here, pl.ds(0 if kind == "left" else width, width)]
                copies.append(pltpu.make_async_copy(src, dst, sem))
    for c in copies:
        c.start()
    for token in done:
        token[...] = jnp.zeros(token.shape, token.dtype)
    for c in copies:
        c.wait()


def load_weights(place, blocks, plan, rows_q, rows_o, model, width, held):
    fresh = held is None
    n = len(blocks)
    return pl.pallas_call(
        functools.partial(load_weights_body, plan, rows_q, rows_o, fresh),
        in_specs=[SMEM] + [ANY] * n + ([] if fresh else [VMEM] * 2),
        out_specs=[VMEM] * (3 if fresh else 2),
        out_shape=[pltpu.VMEM((model, width), BF16), pltpu.VMEM((width, model), BF16)]
        + [jax.ShapeDtypeStruct((8, 128), F32)] * fresh,
        input_output_aliases={} if fresh else {n + 1: 0, n + 2: 1},
        scratch_shapes=[pltpu.SemaphoreType.DMA],
        compiler_params=pltpu.CompilerParams(vmem_limit_bytes=4 * MIB),
        name="load_weights",
    )(place, *[in_hbm(x) for x in blocks], *([] if fresh else held))


def hand_on_body(*refs):
    del refs


def hand_on(arrays, after):
    n = len(arrays)
    return pl.pallas_call(
        hand_on_body,
        in_specs=[ANY] * (n + 1),
        out_specs=[ANY] * n,
        out_shape=[jax.ShapeDtypeStruct(x.shape, x.dtype) for x in arrays],
        input_output_aliases={i: i for i in range(n)},
        compiler_params=pltpu.CompilerParams(vmem_limit_bytes=4 * MIB),
        name="hand_on",
    )(*arrays, after)


def normalise(kv, at, count):
    width = kv.shape[1] // 2
    rows = slice(at, at + count)
    for c in range(0, width, HEAD):
        k = kv[rows, c : c + HEAD].astype(F32)
        r = lax.rsqrt(jnp.mean(k * k, axis=1, keepdims=True) + EPS)
        kv[rows, c : c + HEAD] = (k * r).astype(BF16)


def load_tiles_body(own, before, after, kv, done, sems):
    half = TILE // 2
    places = ((own, 0), (before.at[pl.ds(0, half)], TILE), (after.at[pl.ds(0, half)], 2 * TILE))
    copies = [
        pltpu.make_async_copy(src, kv.at[pl.ds(at, src.shape[0])], sems.at[k])
        for k, (src, at) in enumerate(places)
    ]
    for c in copies:
        c.start()
    done[...] = jnp.zeros(done.shape, done.dtype)
    for c, (src, at) in zip(copies, places):
        c.wait()
        normalise(kv, at, src.shape[0])


def load_low_body(place, before, before_low, after, after_low, held, kv, sems):
    del held
    z, half = place[1], TILE // 2

    def copy(src, at, k):
        return pltpu.make_async_copy(src, kv.at[pl.ds(at, half)], sems.at[k])

    def pick(edge, low, tile, at, k):
        @pl.when(z == edge)
        def _():
            copy(low, at, k).start()

        @pl.when(z != edge)
        def _():
            copy(tile.at[pl.ds(half, half)], at, k).start()

    pick(0, before_low, before, TILE + half, 0)
    pick(NZ - 1, after_low, after, 2 * TILE + half, 1)
    for k, (low, at) in enumerate(((before_low, TILE + half), (after_low, 2 * TILE + half))):
        copy(low, at, k).wait()
        normalise(kv, at, half)


def load_tiles(*tiles):
    return pl.pallas_call(
        load_tiles_body,
        in_specs=[ANY] * 3,
        out_specs=[VMEM] * 2,
        out_shape=[
            pltpu.VMEM((3 * TILE, tiles[0].shape[1]), BF16),
            jax.ShapeDtypeStruct((8, 128), F32),
        ],
        scratch_shapes=[pltpu.SemaphoreType.DMA((3,))],
        compiler_params=pltpu.CompilerParams(vmem_limit_bytes=8 * MIB),
        name="load_tiles",
    )(*[in_hbm(x) for x in tiles])


def load_low(place, tiles, kv):
    return pl.pallas_call(
        load_low_body,
        in_specs=[SMEM] + [ANY] * 4 + [VMEM],
        out_specs=VMEM,
        out_shape=pltpu.VMEM(kv.shape, BF16),
        input_output_aliases={5: 0},
        scratch_shapes=[pltpu.SemaphoreType.DMA((2,))],
        compiler_params=pltpu.CompilerParams(vmem_limit_bytes=8 * MIB),
        name="load_low",
    )(place, *[in_hbm(x) for x in tiles], kv)


def turn_body(
    turn, info, arrived, hidden, wq, wo, kv, scale, shift, gate, gain, mult, *refs
):
    result, written, x_buf, n_buf, q_buf, a_buf, out_buf, in_sem, out_sems = refs[-9:]
    rows, model = x_buf.shape
    width = wq.shape[1]
    section = info[2]
    micro = turn - SKEW * section

    @pl.when(jnp.logical_and(micro >= 0, micro < BATCHES))
    def _():
        row = pl.multiple_of(micro * rows, 16)

        @pl.when(section == 0)
        def _():
            c = pltpu.make_async_copy(hidden.at[pl.ds(row, rows)], x_buf, in_sem)
            c.start()
            c.wait()

        @pl.when(section != 0)
        def _():
            c = pltpu.make_async_copy(arrived.at[pl.ds(0, rows)], x_buf, in_sem)
            c.start()
            c.wait()

        x = x_buf[...].astype(F32)
        centered = x - jnp.mean(x, axis=1, keepdims=True)
        var = jnp.mean(centered * centered, axis=1, keepdims=True)
        n_buf[...] = (centered * lax.rsqrt(var + EPS) * (1.0 + scale[...]) + shift[...]).astype(BF16)
        zero = jnp.zeros((rows, HEAD), BF16)
        two = 2 * HEAD

        def project(c):
            q_buf[:, c : c + two] = jnp.dot(n_buf[...], wq[:, c : c + two], preferred_element_type=F32)

        def unit(c):
            q = q_buf[:, c : c + HEAD]
            r = lax.rsqrt(jnp.mean(q * q, axis=1, keepdims=True) + EPS)
            return (q * r * gain[:, c : c + HEAD]).astype(BF16)

        def score(c):
            pair = jnp.concatenate(
                [
                    jnp.concatenate([unit(c), zero], axis=1),
                    jnp.concatenate([zero, unit(c + HEAD)], axis=1),
                ],
                axis=0,
            )
            return lax.dot_general(
                pair, kv[:, c : c + two], (((1,), (1,)), ((), ())), preferred_element_type=F32
            )

        def mix(c, s):
            e = jnp.exp(s) * mult[...]
            share = 1.0 / jnp.sum(e, axis=1, keepdims=True)
            mixed = jnp.dot(
                e.astype(BF16), kv[:, width + c : width + c + two], preferred_element_type=F32
            )
            a_buf[:, c : c + HEAD] = (mixed[:rows, :HEAD] * share[:rows]).astype(BF16)
            a_buf[:, c + HEAD : c + two] = (mixed[rows:, HEAD:] * share[rows:]).astype(BF16)

        starts = list(range(0, width, two))
        project(starts[0])
        project(starts[1])
        ahead = score(starts[0])
        for i, c in enumerate(starts):
            now = ahead
            if i + 2 < len(starts):
                project(starts[i + 2])
            if i + 1 < len(starts):
                ahead = score(starts[i + 1])
            mix(c, now)
        step = model // OUT_PARTS
        copies = []
        for i, c in enumerate(range(0, model, step)):
            here = pl.ds(c, step)
            branch = jnp.dot(a_buf[...], wo[:, c : c + step], preferred_element_type=F32)
            out_buf[:, c : c + step] = (
                x_buf[:, c : c + step].astype(F32) + gate[:, c : c + step] * branch
            ).astype(BF16)
            for k, dst in enumerate((result.at[:, here], written.at[pl.ds(row, rows), here])):
                copies.append(pltpu.make_async_copy(out_buf.at[:, here], dst, out_sems.at[2 * i + k]))
                copies[-1].start()
        for c in copies:
            c.wait()


def take_turn(turn, info, arrived, hidden, wq, wo, kv, scale, shift, gate, gain, mult, written):
    tokens, model = hidden.shape
    rows = tokens // BATCHES
    width = wq.shape[1]
    keys = kv.shape[0]
    return pl.pallas_call(
        functools.partial(turn_body, turn),
        in_specs=[SMEM, ANY, ANY] + [VMEM] * 8 + [ANY] * len(written),
        out_specs=[ANY, ANY],
        out_shape=[
            jax.ShapeDtypeStruct((rows, model), BF16),
            jax.ShapeDtypeStruct(hidden.shape, BF16),
        ],
        input_output_aliases={11: 1} if written else {},
        scratch_shapes=[
            pltpu.VMEM((rows, model), BF16),
            pltpu.VMEM((rows, model), BF16),
            pltpu.VMEM((rows, width), F32),
            pltpu.VMEM((rows, width), BF16),
            pltpu.VMEM((rows, model), BF16),
            pltpu.SemaphoreType.DMA,
            pltpu.SemaphoreType.DMA((2 * OUT_PARTS,)),
        ],
        compiler_params=pltpu.CompilerParams(vmem_limit_bytes=12 * MIB),
        cost_estimate=pl.CostEstimate(
            flops=4 * rows * width * (model + keys),
            bytes_accessed=26 * MIB,
            transcendentals=rows * keys * (width // HEAD),
        ),
        name="turn",
    )(info, arrived, hidden, wq, wo, kv, scale, shift, gate, gain, mult, *written)


def shards(
    hidden, kv_cache, q_weight, o_weight, mod_shift, mod_scale, mod_gate, q_gain, tile_lists
):
    tokens, model = hidden.shape
    heads = q_gain.shape[1]
    width = heads * HEAD
    rows_q, rows_o = q_weight.shape[1], o_weight.shape[1]
    section = lax.axis_index("segment")
    sections = lax.axis_size("segment")
    seq = lax.axis_index("seq")
    info = jnp.stack([seq // NZ, seq % NZ, section]).astype(jnp.int32)

    own = kv_cache[0]
    z_order, y_order = offsets(NZ), offsets(NY)
    q_own, o_own = q_weight[0], o_weight[0]

    def shard_piece(piece):
        cut = {"q": (q_own, 0), "left": (o_own, 0), "right": (o_own, width)}
        return jnp.concatenate(
            [
                cut[kind][0][at : at + count, cut[kind][1] : cut[kind][1] + width]
                for _, count, kind, at in piece
            ],
            axis=0,
        )

    def send(x, pairs):
        return lax.ppermute(x, "seq", pairs)

    a_z = jnp.concatenate(pieces(ring(shard_piece(A_PIECE), along_z, NZ, A_CUT)), axis=0)
    b_y = jnp.concatenate(pieces(ring(shard_piece(B_PIECE), along_y, NY, B_CUT)), axis=0)
    half = tokens // 2
    edge, b_y = lax.optimization_barrier((own[:half], b_y))
    crossed_up = send(edge, [(y * NZ + NZ - 1, (y + 1) * NZ + NZ - 1) for y in range(NY - 1)])
    crossed_down = send(edge, [((y + 1) * NZ, y * NZ) for y in range(NY - 1)])
    z_here = seq % NZ
    up = jnp.concatenate([jnp.where(z_here == NZ - 1, crossed_up, own[:half]), own[half:]], axis=0)
    down = jnp.concatenate([jnp.where(z_here == 0, crossed_down, own[:half]), own[half:]], axis=0)
    a_z, b_y, up, down = lax.optimization_barrier((a_z, b_y, up, down))
    a_behind, a_ahead = send(a_z, along_y(1)), send(a_z, along_y(-1))
    before, after = send(up, along_z(1)), send(down, along_z(-1))
    b_y, before, after, low_b, low_a = lax.optimization_barrier((b_y, before, after, before[half:], after[half:]))
    before_low = send(low_b, [(y * NZ, (y + 1) * NZ) for y in range(NY - 1)])
    after_low = send(low_a, [((y + 1) * NZ + NZ - 1, y * NZ + NZ - 1) for y in range(NY - 1)])
    b1 = [send(b_y, along_z(1)), send(b_y, along_z(-1))]
    half_a, half_b = a_z.shape[0] // 2, b_y.shape[0] // 2
    quarter = half_a // 2
    parts = (
        a_behind[:quarter], a_ahead[half_a : half_a + quarter],
        a_behind[quarter:half_a], a_ahead[half_a + quarter :],
    )
    *b1, low, high, low2, high2 = lax.optimization_barrier((*b1, *parts))
    a_last = [send(low, along_y(1)), send(high, along_y(-1))]
    *a_last, low2, high2 = lax.optimization_barrier((*a_last, low2, high2))
    a_last += [send(low2, along_y(1)), send(high2, along_y(-1))]
    b2 = [send(b1[0], along_z(1)), send(b1[1], along_z(-1))]

    def a_plan(dy, order):
        return [(dy, dz, A_PIECE, A_ROWS) for dz in order]

    def b_plan(dz, order):
        return [(dy, dz, B_PIECE, B_ROWS) for dy in order]

    sizes = (rows_q, rows_o, model, width)
    few_z, few_y = NZ // 2, NY // 2
    plan = [*[a_plan(d, z_order) for d in (0, -1, 1)], *[b_plan(d, y_order) for d in (0, -1, 1)]]
    *held, token = load_weights(info, [a_z, a_behind, a_ahead, b_y, *b1], plan, *sizes, None)
    b2 = hand_on(b2, token)
    b3 = [send(b2[0], along_z(1)), send(b2[1], along_z(-1))]
    kv, token = load_tiles(own, before, after)
    b3 = hand_on(b3, token)
    b_last = [send(b3[0][:half_b], along_z(1)), send(b3[1][half_b:], along_z(-1))]
    kv = load_low(info, (before, before_low, after, after_low), kv)
    plan = [
        *[b_plan(d, y_order) for d in (-2, 2, -3, 3)],
        *[a_plan(few_y, z_order[k : k + 2]) for k in (0, few_z, 2, few_z + 2)],
        b_plan(few_z, y_order[:few_y]),
        b_plan(few_z, y_order[few_y:]),
    ]
    wq, wo = load_weights(info, [*b2, *b3, *a_last, *b_last], plan, *sizes, held)

    gain = jnp.repeat(q_gain / math.sqrt(HEAD), HEAD, axis=1)
    listed = [jnp.sum((tile_lists[0] == seq + d).astype(F32)) for d in (0, -1, 1)]
    mult = jnp.repeat(jnp.stack(listed)[None], TILE, axis=1)
    written = []
    arrived = [hidden] * SKEW
    for turn in range(SKEW * (sections - 1) + BATCHES):
        result, *written = take_turn(
            turn, info, arrived[turn], hidden, wq, wo, kv, mod_scale, mod_shift, mod_gate, gain, mult, written
        )
        pairs = [(l, l + 1) for l in range(sections - 1) if 0 <= turn - SKEW * l < BATCHES]
        arrived.append(lax.ppermute(result, "segment", pairs) if pairs else result)
    return written[0][None]


def solution(mesh):
    placed = (
        P("seq", None),
        P("segment", "seq", None),
        P("segment", "seq", None),
        P("segment", "seq", None),
        P("segment", None),
        P("segment", None),
        P("segment", None),
        P("segment", None),
        P("seq", None),
    )
    return jax.shard_map(
        shards, mesh=mesh, in_specs=placed, out_specs=P("segment", "seq", None), check_vma=False
    )
```
